32 devices in a mesh: grp: 2 (over y), row: 4 (over z), col: 4 (over x, core).
Axes of the slice: x: 2, y: 2, z: 4, core: 2. Of those that a mesh axis runs over, the one named last changes fastest.
Arguments:
- train_in: bfloat16 [18432, 4096], P(('grp', 'row'), 'col'), parts along dimension 0, may hold values from -6 to 6
- train_grad: bfloat16 [18432, 4096], P(('grp', 'row'), 'col'), parts along dimension 0, may hold values from -6 to 6
- query_in: bfloat16 [3072, 4096], P(('grp', 'row'), 'col'), parts along dimension 0, may hold values from -6 to 6
- query_grad: bfloat16 [3072, 4096], P(('grp', 'row'), 'col'), parts along dimension 0, may hold values from -6 to 6
- proj_in: bfloat16 [4096, 128], P('col'), may hold values from -0.09375 to 0.09375
- proj_out: bfloat16 [4096, 128], P('col'), may hold values from -0.09375 to 0.09375
- inv_fisher: bfloat16 [16384, 16384], P('row', 'col'), may hold values from -0.046875 to 0.046875
- train_len: int32 [384], P(('grp', 'row')), parts along dimension 0, may hold values from 8 to 48, as said below
- query_len: int32 [64], P(('grp', 'row')), parts along dimension 0, may hold values from 8 to 48, as said below
Outputs:
- scores: float32 [32, 384], P(None, ('grp', 'row', 'col')), parts along dimension 1
The draws below stay inside these ranges and needn't reach their ends.
There are 2 independent parts, one for each index of `grp`. The reference program is written for one: setup_inputs(seed, part) draws one part's arguments, and reference() takes and returns one part's arrays. A program takes and returns all parts, laid end to end along the dimension named above; an argument that names none is the same for every part. Nothing has to cross between parts.
Inputs may be any that keep to these rules, and one draw needn't show every extreme that they name: `train_len`: live tokens come first in a cell. Some cell in every draw has all 48 slots live and some has the fewest allowed. `query_len`: live tokens come first in a cell. Some cell in every draw has all 48 slots live and some has the fewest allowed.
All inputs are finite; a program needn't handle non-finite values.
Results may differ from the reference program's by a relative error of at most 0.04.
Values may be sent and summed in bfloat16 or wider, within the bound.
A program may use at most 128 MiB of HBM per device.

```python
import jax
import jax.numpy as jnp
from jax import lax

D = 4096
RANK = 128
CELL = 48
K = 16384
TRAIN = 192
QUERIES = 32
TRAIN_TOK = 9216
QUERY_TOK = 1536
N_ROW = 4
N_COL = 4


def cell_lengths(key, count):
    lowest = max(1, CELL // 6)
    short_key, length_key, full_key, low_key = jax.random.split(key, 4)
    picked = jax.random.randint(short_key, (count,), 0, 2)
    values = jax.random.randint(length_key, (count,), lowest, CELL + 1)
    values = jnp.where(picked == 0, values, jnp.full_like(values, CELL))
    full_pos = jax.random.randint(full_key, (), 0, count)
    low_step = jax.random.randint(low_key, (), 1, count)
    low_pos = (full_pos + low_step) % count
    values = values.at[full_pos].set(CELL).at[low_pos].set(lowest)
    return values.astype(jnp.int32)


def draw_train_len(key, part):
    return cell_lengths(jax.random.fold_in(key, 11), TRAIN)


def draw_query_len(key, part):
    return cell_lengths(jax.random.fold_in(key, 23), QUERIES)


def shard_levels(stream_key, shape, cuts, low, top_value):
    factor_of = 1.0
    for dim, parts in cuts:
        heights = jax.random.uniform(jax.random.fold_in(jax.random.fold_in(stream_key, 6), dim), (parts,), jnp.float32, low / len(cuts), top_value / len(cuts))
        factor_of = factor_of * jnp.repeat(jnp.exp(heights), shape[dim] // parts).reshape((-1,) + (1,) * (len(shape) - 1 - dim))
    return factor_of


def noise(stream_key, extent, deviation, bound, cuts=(), kind=jnp.bfloat16):
    entries = jax.random.normal(stream_key, extent, jnp.float32) * deviation
    if len(cuts) > 0:
        entries = shard_levels(stream_key, extent, cuts, -0.22, 0.18) * entries
    return jnp.clip(entries, min=-bound, max=bound).astype(kind)


def setup_inputs(seed: int = 0, part: int = 0) -> dict:
    streams_of = jax.random.split(jax.random.key(seed), 10)
    own_keys = jax.random.split(jax.random.fold_in(streams_of[9], part), 10)
    train_in = noise(own_keys[0], (TRAIN_TOK, D), 1.0, 6.0, ((0, 4), (1, 4)))
    train_grad = noise(own_keys[1], (TRAIN_TOK, D), 1.0, 6.0, ((0, 4), (1, 4)))
    query_in = noise(own_keys[2], (QUERY_TOK, D), 1.0, 6.0, ((0, 4), (1, 4)))
    query_grad = noise(own_keys[3], (QUERY_TOK, D), 1.0, 6.0, ((0, 4), (1, 4)))
    proj_in = noise(streams_of[4], (D, RANK), D ** -0.5, 0.09375, ((0, 4),))
    proj_out = noise(streams_of[5], (D, RANK), D ** -0.5, 0.09375, ((0, 4),))
    inv_fisher = noise(streams_of[6], (K, K), K ** -0.5, 0.046875, ((0, 4), (1, 4)))
    train_len = draw_train_len(jax.random.fold_in(jax.random.fold_in(streams_of[9], part), 71), part)
    query_len = draw_query_len(jax.random.fold_in(jax.random.fold_in(streams_of[9], part), 71), part)
    return dict(train_in=train_in, train_grad=train_grad, query_in=query_in, query_grad=query_grad, proj_in=proj_in, proj_out=proj_out, inv_fisher=inv_fisher, train_len=train_len, query_len=query_len)


def project(data, proj):
    width = data.shape[1] // N_COL
    total = jnp.zeros((data.shape[0], proj.shape[1]), jnp.float32)
    for block in range(N_COL):
        block_data = data[:, block * width:(block + 1) * width].astype(jnp.float32)
        block_proj = proj[block * width:(block + 1) * width].astype(jnp.float32)
        product = jnp.dot(block_data, block_proj, preferred_element_type=jnp.float32)
        rounded = lax.optimization_barrier(product.astype(jnp.bfloat16))
        total = total + rounded.astype(jnp.float32)
    return total


def live_weights(lengths):
    position = jnp.arange(CELL, dtype=jnp.int32)[None, :]
    scale = 1.0 / lengths[:, None].astype(jnp.float32)
    weight = jnp.where(position < lengths[:, None], scale, jnp.zeros_like(scale))
    return weight.reshape(-1, 1)


def outer_sums(back, acts, count):
    back_cells = back.reshape(count, CELL, -1).astype(jnp.float32)
    acts_cells = acts.reshape(count, CELL, -1).astype(jnp.float32)
    gram = jnp.einsum('eta,etb->eab', back_cells, acts_cells)
    return gram.reshape(count, -1).astype(jnp.bfloat16)


def reference(train_in, train_grad, query_in, query_grad, proj_in, proj_out, inv_fisher, train_len, query_len):
    train_acts = project(train_in, proj_in)
    train_back = project(train_grad, proj_out)
    query_acts = project(query_in, proj_in)
    query_back = project(query_grad, proj_out)
    train_back_w = (train_back * live_weights(train_len)).astype(jnp.bfloat16)
    query_back_w = (query_back * live_weights(query_len)).astype(jnp.bfloat16)
    grads = outer_sums(train_back_w, train_acts.astype(jnp.bfloat16), TRAIN)
    query_grads = outer_sums(query_back_w, query_acts.astype(jnp.bfloat16), QUERIES)
    query_wide = query_grads.astype(jnp.float32)
    fisher_blocks = inv_fisher.reshape(N_ROW, K // N_ROW, K)

    def apply_block(block):
        return lax.dot_general(query_wide, block.astype(jnp.float32), (((1,), (1,)), ((), ())), preferred_element_type=jnp.float32)

    pre_blocks = lax.map(apply_block, fisher_blocks)
    pre = jnp.transpose(pre_blocks, (1, 0, 2)).reshape(QUERIES, K).astype(jnp.bfloat16)
    scores = lax.dot_general(pre.astype(jnp.float32), grads.astype(jnp.float32), (((1,), (1,)), ((), ())), preferred_element_type=jnp.float32)
    return scores
```

```python
import functools

import jax
import jax.numpy as jnp
from jax import lax
from jax.experimental import pallas as pl
from jax.experimental.pallas import tpu as pltpu
from jax.sharding import PartitionSpec as P

CELL = 48
F32 = jnp.float32
BF16 = jnp.bfloat16
MESH = pl.DeviceIdType.MESH


def token_weights(lens, base, count):
    tok = lax.broadcasted_iota(jnp.int32, (1, count * CELL), 1)
    length = jnp.ones_like(tok)
    start = jnp.zeros_like(tok)
    for e in range(count):
        here = tok >= e * CELL
        length = jnp.where(here, lens[base + e], length)
        start = jnp.where(here, e * CELL, start)
    scale = 1.0 / length.astype(F32)
    return jnp.where(tok - start < length, scale, jnp.zeros_like(scale))


def kernel(
    R, C,
    train_in, train_grad, query_in, query_grad, proj_in, proj_out, fisher, train_len, query_len,
    out,
    tin, tgr, qin, qgr, pin, pout, fbuf,
    qa_send, qa_recv, qb_send, qb_recv, gath, gt,
    t_send, t_recv, bw, g_send, g_recv, p_send, p_recv, s_send, s_recv,
    lsem, tsem, fsem, qas, qar, qbs, qbr, gs, gr, ts, tr, ggs, ggr, ps, pr, ss, sr,
):
    r = lax.axis_index("row")
    c = lax.axis_index("col")
    N = R * C
    QT, RANK = qa_send.shape
    QC = QT // CELL
    OT = tin.shape[1]
    owned = OT // CELL
    band = qb_send.shape[1]
    Q = R * QC
    KC = fbuf.shape[1]
    ka = bw.shape[1]
    kb = KC // ka

    def row_at(i):
        return lax.rem(r + i, R)

    def col_at(i):
        return lax.rem(c + i, C)

    def remote(src, dst, send, recv, rr, cc):
        return pltpu.make_async_remote_copy(
            src_ref=src, dst_ref=dst, send_sem=send, recv_sem=recv,
            device_id={"row": rr, "col": cc}, device_id_type=MESH,
        )

    def peer(n):
        return lax.rem(r + n // C, R), lax.rem(c + n % C, C)

    def back_peer(n):
        return lax.rem(r + R - n // C, R), lax.rem(c + C - n % C, C)

    loads = [
        pltpu.make_async_copy(a, b, lsem.at[i])
        for i, (a, b) in enumerate(
            [(query_in, qin), (proj_in, pin), (query_grad, qgr), (proj_out, pout)]
        )
    ]
    for load in loads:
        load.start()

    barrier = pltpu.get_barrier_semaphore()

    @pl.loop(1, N)
    def _(n):
        rr, cc = peer(n)
        pl.semaphore_signal(barrier, inc=1, device_id={"row": rr, "col": cc}, device_id_type=MESH)

    order = list(range(1, C)) + [0]
    tloads = {}
    for i in order:
        rows = pl.ds(pl.multiple_of(col_at(i) * OT, 16), OT)
        tloads[i] = (
            pltpu.make_async_copy(train_in.at[rows], tin.at[i], tsem.at[0, i]),
            pltpu.make_async_copy(train_grad.at[rows], tgr.at[i], tsem.at[1, i]),
        )
        tloads[i][0].start()
        tloads[i][1].start()

    loads[0].wait()
    loads[1].wait()
    qa_send[...] = jnp.dot(qin[...], pin[...], preferred_element_type=F32).astype(BF16)
    pl.semaphore_wait(barrier, N - 1)
    qa = [None] + [
        remote(qa_send, qa_recv.at[i], qas.at[i], qar.at[i], r, col_at(i)) for i in range(1, C)
    ]
    for i in range(1, C):
        qa[i].start()
    loads[2].wait()
    loads[3].wait()
    back = jnp.dot(qgr[...], pout[...], preferred_element_type=F32)
    back_t = back.T.astype(BF16)
    for i in range(C):
        qb_send[i] = back_t[i * band:(i + 1) * band]
    qb = [None] + [
        remote(qb_send.at[col_at(i)], qb_recv.at[i], qbs.at[i], qbr.at[i], r, col_at(i))
        for i in range(1, C)
    ]
    for i in range(1, C):
        qb[i].start()

    floads = {}
    for i in order:
        rows = pl.ds(pl.multiple_of(col_at(i) * KC, 16), KC)
        floads[i] = pltpu.make_async_copy(fisher.at[rows], fbuf.at[i], fsem.at[i])
        floads[i].start()

    tc = {}
    for i in order:
        tloads[i][0].wait()
        t_send[i, 0] = jnp.dot(tin[i], pin[...], preferred_element_type=F32).astype(BF16)
        tloads[i][1].wait()
        t_send[i, 1] = jnp.dot(tgr[i], pout[...], preferred_element_type=F32).astype(BF16)
        if i:
            tc[i] = remote(t_send.at[i], t_recv.at[i], ts.at[i], tr.at[i], r, col_at(i))
            tc[i].start()

    acts = qa_send[...].astype(F32)
    for i in range(1, C):
        qa[i].wait_recv()
        acts = acts + qa_recv[i].astype(F32)
    backs = qb_send[c].astype(F32)
    for i in range(1, C):
        qb[i].wait_recv()
        backs = backs + qb_recv[i].astype(F32)
    backs = (backs * token_weights(query_len, 0, QC)).astype(BF16)
    pick = lax.broadcasted_iota(jnp.int32, (band, QC, band), 0) == lax.broadcasted_iota(
        jnp.int32, (band, QC, band), 2
    )
    pick = jnp.where(pick, 1.0, 0.0).reshape(band * QC, band).astype(BF16)
    spread = jnp.dot(pick, backs, preferred_element_type=F32).reshape(band, QC, QT)
    first = lax.broadcasted_iota(jnp.int32, (band, QC, QT), 1) * CELL
    tok = lax.broadcasted_iota(jnp.int32, (band, QC, QT), 2)
    spread = jnp.where((tok >= first) & (tok < first + CELL), spread, 0.0)
    gath[r] = jnp.dot(
        spread.reshape(band * QC, QT).astype(BF16), acts.astype(BF16), preferred_element_type=F32
    ).astype(BF16)
    gc = [None] + [
        remote(gath.at[r], gath.at[r], gs.at[i], gr.at[i], row_at(i), c) for i in range(1, R)
    ]
    for i in range(1, R):
        gc[i].start()

    t_acts = t_send[0, 0].astype(F32)
    t_back = t_send[0, 1].astype(F32)
    for i in range(1, C):
        tc[i].wait_recv()
        t_acts = t_acts + t_recv[i, 0].astype(F32)
        t_back = t_back + t_recv[i, 1].astype(F32)
    t_acts = t_acts.astype(BF16)
    weight = token_weights(train_len, c * owned, owned)
    t_back = (t_back.T * weight).astype(BF16).astype(F32)
    halves = RANK // kb
    for n in range(N):
        a0 = n * KC // RANK
        bw[n] = t_back[a0:a0 + ka]
    first = lax.broadcasted_iota(jnp.int32, (owned, ka, OT), 0) * CELL
    tok = lax.broadcasted_iota(jnp.int32, (owned, ka, OT), 2)
    live = (tok >= first) & (tok < first + CELL)

    def grads_for(chunk):
        lhs = jnp.where(live, bw[chunk][None], 0.0).reshape(owned * ka, OT).astype(BF16)
        both = jnp.dot(lhs, t_acts, preferred_element_type=F32)
        if halves == 1:
            return both.astype(BF16)
        value = both[:, :kb]
        for h in range(1, halves):
            value = jnp.where(lax.rem(chunk, halves) == h, both[:, h * kb:(h + 1) * kb], value)
        return value.astype(BF16)

    def grads_copy(n):
        rr, cc = peer(n)
        return remote(g_send.at[n], g_recv.at[n], ggs.at[n], ggr.at[n], rr, cc)

    g_recv[0] = grads_for(r * C + c)

    @pl.loop(1, N)
    def _(n):
        rr, cc = peer(n)
        g_send[n] = grads_for(rr * C + cc)
        grads_copy(n).start()

    for i in range(1, R):
        here = lax.rem(r + R - i, R)
        remote(gath.at[here], gath.at[here], gs.at[i], gr.at[i], row_at(i), c).wait_recv()
    whole = gath[...].astype(F32)
    for a in range(band):
        rows = [whole[i, a * QC:(a + 1) * QC] for i in range(R)]
        gt[a * RANK:(a + 1) * RANK] = jnp.concatenate(rows, 0).T.astype(BF16)

    pc = {}
    for i in order:
        floads[i].wait()
        part = jnp.dot(fbuf[i], gt[...], preferred_element_type=F32).astype(BF16)
        for a in range(ka):
            p_send[i, :, a * Q:(a + 1) * Q] = part[a * kb:(a + 1) * kb]
        if i:
            pc[i] = remote(p_send.at[i], p_recv.at[i], ps.at[i], pr.at[i], r, col_at(i))
            pc[i].start()
    pre = p_send[0].astype(F32)
    for i in range(1, C):
        pc[i].wait_recv()
        pre = pre + p_recv[i].astype(F32)
    pre = pre.astype(BF16)

    @pl.loop(1, N)
    def _(n):
        grads_copy(n).wait_recv()

    lhs = g_recv[...].reshape(N * owned * ka, kb)
    every = jnp.dot(lhs, pre, preferred_element_type=F32).reshape(N, owned, ka, ka * Q)
    lane = lax.broadcasted_iota(jnp.int32, (N, owned, ka, ka * Q), 3)
    low = lax.broadcasted_iota(jnp.int32, (N, owned, ka, ka * Q), 2) * Q
    every = jnp.sum(jnp.where((lane >= low) & (lane < low + Q), every, 0.0), axis=2)
    value = every[:, :, :Q]
    for a in range(1, ka):
        value = value + every[:, :, a * Q:(a + 1) * Q]
    s_send[...] = value

    def score_copy(n):
        rr, cc = back_peer(n)
        return remote(s_send.at[n], s_recv.at[n], ss.at[n], sr.at[n], rr, cc)

    @pl.loop(1, N)
    def _(n):
        score_copy(n).start()

    @pl.loop(1, N)
    def _(n):
        score_copy(n).wait_recv()

    s_recv[0] = s_send[0]
    out[...] = jnp.sum(s_recv[...], axis=0)

    for i in range(1, C):
        qa[i].wait_send()
        qb[i].wait_send()
        tc[i].wait_send()
        pc[i].wait_send()
    for i in range(1, R):
        gc[i].wait_send()

    @pl.loop(1, N)
    def _(n):
        grads_copy(n).wait_send()
        score_copy(n).wait_send()


def body(R, C, *args):
    train_in, train_grad, query_in, query_grad, proj_in, proj_out, fisher, train_len, query_len = args
    T, D = train_in.shape
    QT = query_in.shape[0]
    rank = proj_in.shape[1]
    K1, J = fisher.shape
    N = R * C
    OT = T // C
    owned = OT // CELL
    QC = QT // CELL
    Q = R * QC
    band = rank // C
    KC = K1 // C
    ka = max(1, KC // rank)
    kb = KC // ka
    dma = pltpu.SemaphoreType.DMA
    scratch = [
        pltpu.VMEM((C, OT, D), BF16),
        pltpu.VMEM((C, OT, D), BF16),
        pltpu.VMEM((QT, D), BF16),
        pltpu.VMEM((QT, D), BF16),
        pltpu.VMEM((D, rank), BF16),
        pltpu.VMEM((D, rank), BF16),
        pltpu.VMEM((C, KC, J), BF16),
        pltpu.VMEM((QT, rank), BF16),
        pltpu.VMEM((C, QT, rank), BF16),
        pltpu.VMEM((C, band, QT), BF16),
        pltpu.VMEM((C, band, QT), BF16),
        pltpu.VMEM((R, band * QC, rank), BF16),
        pltpu.VMEM((J, Q), BF16),
        pltpu.VMEM((C, 2, OT, rank), BF16),
        pltpu.VMEM((C, 2, OT, rank), BF16),
        pltpu.VMEM((N, ka, OT), F32),
        pltpu.VMEM((N, owned * ka, kb), BF16),
        pltpu.VMEM((N, owned * ka, kb), BF16),
        pltpu.VMEM((C, kb, ka * Q), BF16),
        pltpu.VMEM((C, kb, ka * Q), BF16),
        pltpu.VMEM((N, owned, Q), F32),
        pltpu.VMEM((N, owned, Q), F32),
        dma((4,)), dma((2, C)), dma((C,)),
        dma((C,)), dma((C,)), dma((C,)), dma((C,)),
        dma((R,)), dma((R,)),
        dma((C,)), dma((C,)),
        dma((N,)), dma((N,)),
        dma((C,)), dma((C,)),
        dma((N,)), dma((N,)),
    ]
    flops = 2 * rank * D * 2 * (T + QT) + 2 * Q * K1 * J
    scores = pl.pallas_call(
        functools.partial(kernel, R, C),
        out_shape=jax.ShapeDtypeStruct((owned, Q), F32),
        in_specs=[pl.BlockSpec(memory_space=pl.ANY)] * 7
        + [pl.BlockSpec(memory_space=pltpu.SMEM)] * 2,
        out_specs=pl.BlockSpec(memory_space=pltpu.VMEM),
        scratch_shapes=scratch,
        compiler_params=pltpu.CompilerParams(
            collective_id=0, has_side_effects=True, vmem_limit_bytes=60 * 2**20
        ),
        cost_estimate=pl.CostEstimate(
            flops=flops, bytes_accessed=2 * (K1 * J + 2 * D * (T + QT + rank)), transcendentals=0
        ),
    )(*args)
    return scores.T


def solution(mesh):
    cells = P(("grp", "row"))
    data = P(("grp", "row"), "col")
    proj = P("col", None)
    in_specs = (data, data, data, data, proj, proj, P("row", "col"), cells, cells)
    run = functools.partial(body, mesh.shape["row"], mesh.shape["col"])
    return jax.shard_map(
        run, mesh=mesh, in_specs=in_specs, out_specs=P(None, ("grp", "row", "col")), check_vma=False
    )
```

```python
import functools

import jax
import jax.numpy as jnp
from jax import lax
from jax.experimental import pallas as pl
from jax.experimental.pallas import tpu as pltpu
from jax.sharding import PartitionSpec as P

CELL = 48
F32 = jnp.float32
BF16 = jnp.bfloat16
MESH = pl.DeviceIdType.MESH


def dot2(a, b):
    half = a.shape[0] // 32 * 16
    if half == 0:
        return jnp.dot(a, b, preferred_element_type=F32)
    top = jnp.dot(a[:half], b, preferred_element_type=F32)
    low = jnp.dot(a[half:], b, preferred_element_type=F32)
    return jnp.concatenate([top, low], 0)


def token_weights(lens, base, count):
    tok = lax.broadcasted_iota(jnp.int32, (1, count * CELL), 1)
    length = jnp.ones_like(tok)
    start = jnp.zeros_like(tok)
    for e in range(count):
        here = tok >= e * CELL
        length = jnp.where(here, lens[base + e], length)
        start = jnp.where(here, e * CELL, start)
    scale = 1.0 / length.astype(F32)
    return jnp.where(tok - start < length, scale, jnp.zeros_like(scale))


def kernel(
    R, C, G,
    train_in, train_grad, query_in, query_grad, proj_in, proj_out, fisher, train_len, query_len,
    out,
    tin, tgr, qin, qgr, pin, pout, fbuf,
    qa_send, qa_recv, qb_send, qb_recv, gath, gt,
    t_send, t1_recv, t2_recv, bw, g_send, g_recv, p_send, p_recv, s_send, s_recv,
    lsem, tsem, fsem, qas, qar, qbs, qbr, gs, gr, ts, t1r, t2r, ggs, ggr, ps, pr, ss, sr,
):
    r = lax.axis_index("row")
    c = lax.axis_index("col")
    N = R * C
    QT, RANK = qa_send.shape
    QC = QT // CELL
    OT = tin.shape[1]
    owned = OT // CELL
    band = qb_send.shape[1]
    Q = R * QC
    KC = fbuf.shape[1]
    ka = bw.shape[1]
    kb = KC // ka

    def row_at(i):
        return lax.rem(r + i, R)

    def col_at(i):
        return lax.rem(c + i, C)

    def remote(src, dst, send, recv, rr, cc):
        return pltpu.make_async_remote_copy(
            src_ref=src, dst_ref=dst, send_sem=send, recv_sem=recv,
            device_id={"row": rr, "col": cc}, device_id_type=MESH,
        )

    def peer(n):
        return lax.rem(r + n // C, R), lax.rem(c + n % C, C)

    def back_peer(n):
        return lax.rem(r + R - n // C, R), lax.rem(c + C - n % C, C)

    loads = [
        pltpu.make_async_copy(a, b, lsem.at[i])
        for i, (a, b) in enumerate(
            [(query_in, qin), (proj_in, pin), (query_grad, qgr), (proj_out, pout)]
        )
    ]
    for load in loads:
        load.start()

    barrier = pltpu.get_barrier_semaphore()

    @pl.loop(1, N)
    def _(n):
        rr, cc = peer(n)
        pl.semaphore_signal(barrier, inc=1, device_id={"row": rr, "col": cc}, device_id_type=MESH)

    order = list(range(1, C)) + [0]
    X = C // G
    torder = [(j, s) for s in range(G) for j in list(range(1, X)) + [0]]
    chip, core = c // G, lax.rem(c, G)
    tloads = {}
    for j, s in torder:
        i = s * X + j
        owner = lax.rem(chip + j, X) * G + lax.rem(core + 1 + s, G)
        rows = pl.ds(pl.multiple_of(owner * OT, 16), OT)
        tloads[i] = (
            pltpu.make_async_copy(train_in.at[rows], tin.at[i], tsem.at[0, i]),
            pltpu.make_async_copy(train_grad.at[rows], tgr.at[i], tsem.at[1, i]),
        )
        tloads[i][0].start()
        tloads[i][1].start()

    loads[0].wait()
    loads[1].wait()
    qa_send[...] = dot2(qin[...], pin[...]).astype(BF16)
    pl.semaphore_wait(barrier, N - 1)
    qa = [None] + [
        remote(qa_send, qa_recv.at[i], qas.at[i], qar.at[i], r, col_at(i)) for i in range(1, C)
    ]
    for i in range(1, C):
        qa[i].start()
    loads[2].wait()
    loads[3].wait()
    back = dot2(qgr[...], pout[...])
    back_t = back.T.astype(BF16)
    for i in range(C):
        qb_send[i] = back_t[i * band:(i + 1) * band]
    qb = [None] + [
        remote(qb_send.at[col_at(i)], qb_recv.at[i], qbs.at[i], qbr.at[i], r, col_at(i))
        for i in range(1, C)
    ]
    for i in range(1, C):
        qb[i].start()

    floads = {}
    for i in order:
        rows = pl.ds(pl.multiple_of(col_at(i) * KC, 16), KC)
        floads[i] = pltpu.make_async_copy(fisher.at[rows], fbuf.at[i], fsem.at[i])
        floads[i].start()

    t1 = {}
    t2 = {}
    mate = chip * G + lax.rem(core + 1, G)
    for j, s in torder:
        i = s * X + j
        tloads[i][0].wait()
        left = dot2(tin[i], pin[...])
        tloads[i][1].wait()
        right = dot2(tgr[i], pout[...])
        if s < G - 1:
            t_send[i, 0] = left.astype(BF16)
            t_send[i, 1] = right.astype(BF16)
            t1[j] = remote(t_send.at[i], t1_recv.at[j], ts.at[i], t1r.at[j], r, mate)
            t1[j].start()
            continue
        t_send[i, 0] = left.astype(BF16)
        t_send[i, 1] = right.astype(BF16)
    for j in list(range(1, X)) + [0]:
        i = (G - 1) * X + j
        if G > 1:
            t1[j].wait_recv()
            if j:
                t_send[i] = (t_send[i].astype(F32) + t1_recv[j].astype(F32)).astype(BF16)
        if j:
            far = lax.rem(chip + j, X) * G + core
            t2[j] = remote(t_send.at[i], t2_recv.at[j], ts.at[i], t2r.at[j], r, far)
            t2[j].start()

    acts = qa_send[...].astype(F32)
    for i in range(1, C):
        qa[i].wait_recv()
        acts = acts + qa_recv[i].astype(F32)
    backs = qb_send[c].astype(F32)
    for i in range(1, C):
        qb[i].wait_recv()
        backs = backs + qb_recv[i].astype(F32)
    backs = (backs * token_weights(query_len, 0, QC)).astype(BF16)
    pick = lax.broadcasted_iota(jnp.int32, (band, QC, band), 0) == lax.broadcasted_iota(
        jnp.int32, (band, QC, band), 2
    )
    pick = jnp.where(pick, 1.0, 0.0).reshape(band * QC, band).astype(BF16)
    spread = jnp.dot(pick, backs, preferred_element_type=F32).reshape(band, QC, QT)
    first = lax.broadcasted_iota(jnp.int32, (band, QC, QT), 1) * CELL
    tok = lax.broadcasted_iota(jnp.int32, (band, QC, QT), 2)
    spread = jnp.where((tok >= first) & (tok < first + CELL), spread, 0.0)
    gath[r] = jnp.dot(
        spread.reshape(band * QC, QT).astype(BF16), acts.astype(BF16), preferred_element_type=F32
    ).astype(BF16)
    gc = [None] + [
        remote(gath.at[r], gath.at[r], gs.at[i], gr.at[i], row_at(i), c) for i in range(1, R)
    ]
    for i in range(1, R):
        gc[i].start()

    for i in range(1, R):
        here = lax.rem(r + R - i, R)
        remote(gath.at[here], gath.at[here], gs.at[i], gr.at[i], row_at(i), c).wait_recv()
    whole = gath[...].astype(F32)
    for a in range(band):
        rows = [whole[i, a * QC:(a + 1) * QC] for i in range(R)]
        gt[a * RANK:(a + 1) * RANK] = jnp.concatenate(rows, 0).T.astype(BF16)

    pc = {}

    def fisher_chunk(i):
        floads[i].wait()
        part = dot2(fbuf[i], gt[...]).astype(BF16)
        for a in range(ka):
            p_send[i, :, a * Q:(a + 1) * Q] = part[a * kb:(a + 1) * kb]
        if i:
            pc[i] = remote(p_send.at[i], p_recv.at[i], ps.at[i], pr.at[i], r, col_at(i))
            pc[i].start()

    early = max(1, C // 4)
    for i in order[:early]:
        fisher_chunk(i)

    own = (G - 1) * X
    t_sum = t_send[own].astype(F32)
    if G > 1:
        t_sum = t_sum + t1_recv[0].astype(F32)
    for j in range(1, X):
        t2[j].wait_recv()
        t_sum = t_sum + t2_recv[j].astype(F32)
    t_acts, t_back = t_sum[0], t_sum[1]
    t_acts = t_acts.astype(BF16)
    weight = token_weights(train_len, c * owned, owned)
    t_back = (t_back.T * weight).astype(BF16).astype(F32)
    halves = RANK // kb
    for n in range(N):
        a0 = n * KC // RANK
        bw[n] = t_back[a0:a0 + ka]
    first = lax.broadcasted_iota(jnp.int32, (owned, ka, OT), 0) * CELL
    tok = lax.broadcasted_iota(jnp.int32, (owned, ka, OT), 2)
    live = (tok >= first) & (tok < first + CELL)

    def grads_for(chunk):
        lhs = jnp.where(live, bw[chunk][None], 0.0).reshape(owned * ka, OT).astype(BF16)
        both = jnp.dot(lhs, t_acts, preferred_element_type=F32)
        if halves == 1:
            return both.astype(BF16)
        value = both[:, :kb]
        for h in range(1, halves):
            value = jnp.where(lax.rem(chunk, halves) == h, both[:, h * kb:(h + 1) * kb], value)
        return value.astype(BF16)

    def grads_copy(n):
        rr, cc = peer(n)
        return remote(g_send.at[n], g_recv.at[n], ggs.at[n], ggr.at[n], rr, cc)

    U = 4 if N % 4 == 0 else 1
    values = []
    for n in range(U):
        rr, cc = peer(n)
        values.append(grads_for(rr * C + cc))
    g_recv[0] = values[0]
    for n in range(1, U):
        g_send[n] = values[n]
        grads_copy(n).start()

    @pl.loop(1, N // U)
    def _(m):
        values = []
        for u in range(U):
            rr, cc = peer(m * U + u)
            values.append(grads_for(rr * C + cc))
        for u in range(U):
            g_send[m * U + u] = values[u]
        for u in range(U):
            grads_copy(m * U + u).start()

    for i in order[early:]:
        fisher_chunk(i)
    pre = p_send[0].astype(F32)
    for i in range(1, C):
        pc[i].wait_recv()
        pre = pre + p_recv[i].astype(F32)
    pre = pre.astype(BF16)

    @pl.loop(1, N)
    def _(n):
        grads_copy(n).wait_recv()

    lhs = g_recv[...].reshape(N * owned * ka, kb)
    every = jnp.dot(lhs, pre, preferred_element_type=F32).reshape(N, owned, ka, ka * Q)
    lane = lax.broadcasted_iota(jnp.int32, (N, owned, ka, ka * Q), 3)
    low = lax.broadcasted_iota(jnp.int32, (N, owned, ka, ka * Q), 2) * Q
    every = jnp.sum(jnp.where((lane >= low) & (lane < low + Q), every, 0.0), axis=2)
    value = every[:, :, :Q]
    for a in range(1, ka):
        value = value + every[:, :, a * Q:(a + 1) * Q]
    s_send[...] = value

    def score_copy(n):
        rr, cc = back_peer(n)
        return remote(s_send.at[n], s_recv.at[n], ss.at[n], sr.at[n], rr, cc)

    @pl.loop(1, N)
    def _(n):
        score_copy(n).start()

    @pl.loop(1, N)
    def _(n):
        score_copy(n).wait_recv()

    s_recv[0] = s_send[0]
    out[...] = jnp.sum(s_recv[...], axis=0)

    for i in range(1, C):
        qa[i].wait_send()
        qb[i].wait_send()
        pc[i].wait_send()
    for copy in list(t1.values()) + list(t2.values()):
        copy.wait_send()
    for i in range(1, R):
        gc[i].wait_send()

    @pl.loop(1, N)
    def _(n):
        grads_copy(n).wait_send()
        score_copy(n).wait_send()


def body(R, C, *args):
    train_in, train_grad, query_in, query_grad, proj_in, proj_out, fisher, train_len, query_len = args
    T, D = train_in.shape
    QT = query_in.shape[0]
    rank = proj_in.shape[1]
    K1, J = fisher.shape
    N = R * C
    G = 2 if C % 2 == 0 else 1
    OT = T // C
    owned = OT // CELL
    QC = QT // CELL
    Q = R * QC
    band = rank // C
    KC = K1 // C
    ka = max(1, KC // rank)
    kb = KC // ka
    dma = pltpu.SemaphoreType.DMA
    scratch = [
        pltpu.VMEM((C, OT, D), BF16),
        pltpu.VMEM((C, OT, D), BF16),
        pltpu.VMEM((QT, D), BF16),
        pltpu.VMEM((QT, D), BF16),
        pltpu.VMEM((D, rank), BF16),
        pltpu.VMEM((D, rank), BF16),
        pltpu.VMEM((C, KC, J), BF16),
        pltpu.VMEM((QT, rank), BF16),
        pltpu.VMEM((C, QT, rank), BF16),
        pltpu.VMEM((C, band, QT), BF16),
        pltpu.VMEM((C, band, QT), BF16),
        pltpu.VMEM((R, band * QC, rank), BF16),
        pltpu.VMEM((J, Q), BF16),
        pltpu.VMEM((C, 2, OT, rank), BF16),
        pltpu.VMEM((C // G, 2, OT, rank), BF16),
        pltpu.VMEM((C // G, 2, OT, rank), BF16),
        pltpu.VMEM((N, ka, OT), F32),
        pltpu.VMEM((N, owned * ka, kb), BF16),
        pltpu.VMEM((N, owned * ka, kb), BF16),
        pltpu.VMEM((C, kb, ka * Q), BF16),
        pltpu.VMEM((C, kb, ka * Q), BF16),
        pltpu.VMEM((N, owned, Q), F32),
        pltpu.VMEM((N, owned, Q), F32),
        dma((4,)), dma((2, C)), dma((C,)),
        dma((C,)), dma((C,)), dma((C,)), dma((C,)),
        dma((R,)), dma((R,)),
        dma((C,)), dma((C // G,)), dma((C // G,)),
        dma((N,)), dma((N,)),
        dma((C,)), dma((C,)),
        dma((N,)), dma((N,)),
    ]
    flops = 2 * rank * D * 2 * (T + QT) + 2 * Q * K1 * J
    scores = pl.pallas_call(
        functools.partial(kernel, R, C, G),
        out_shape=jax.ShapeDtypeStruct((owned, Q), F32),
        in_specs=[pl.BlockSpec(memory_space=pl.ANY)] * 7
        + [pl.BlockSpec(memory_space=pltpu.SMEM)] * 2,
        out_specs=pl.BlockSpec(memory_space=pltpu.VMEM),
        scratch_shapes=scratch,
        compiler_params=pltpu.CompilerParams(
            collective_id=0, has_side_effects=True, vmem_limit_bytes=60 * 2**20
        ),
        cost_estimate=pl.CostEstimate(
            flops=flops, bytes_accessed=2 * (K1 * J + 2 * D * (T + QT + rank)), transcendentals=0
        ),
    )(*args)
    return scores.T


def solution(mesh):
    cells = P(("grp", "row"))
    data = P(("grp", "row"), "col")
    proj = P("col", None)
    in_specs = (data, data, data, data, proj, proj, P("row", "col"), cells, cells)
    run = functools.partial(body, mesh.shape["row"], mesh.shape["col"])
    return jax.shard_map(
        run, mesh=mesh, in_specs=in_specs, out_specs=P(None, ("grp", "row", "col")), check_vma=False
    )
```
